256 devices in a mesh: seq: 32 (over z, y), fsdp: 8 (over x, core).
Axes of the slice: x: 4, y: 4, z: 8, core: 2. Of those that a mesh axis runs over, the one named last changes fastest.
Arguments:
- x_tokens: bfloat16 [20480, 5120], P('seq', 'fsdp'), may hold values from -6 to 6
- w_qkv: bfloat16 [3, 5120, 5120], P(None, 'seq', 'fsdp'), may hold values from -0.078125 to 0.078125
- q_gain: float32 [5120], P('fsdp'), may hold values from 0.5 to 6
- k_gain: float32 [5120], P('fsdp'), may hold values from 0.5 to 6
- head_kind: int32 [40], P('fsdp'), may hold values from 0 to 1, as said below
- block_live: int32 [32, 40, 5, 5], P('seq', 'fsdp'), may hold values from 0 to 1, as said below
Outputs:
- attended: bfloat16 [20480, 5120], P('seq', 'fsdp')
The draws below stay inside these ranges and needn't reach their ends.
Inputs may be any that keep to these rules, and one draw needn't show every extreme that they name: `head_kind`: each aligned block of 5 consecutive heads holds exactly 2 heads labelled 1. block_live[f, h, i, i] is 1 for every frame, head and block i.
All inputs are finite; a program needn't handle non-finite values.
Results may differ from the reference program's by a relative error of at most 0.006.
The reference program's roundings to bfloat16 on the way (of `values`, `sp_weights`, `spatial`, `tm_weights` and `temporal`) count: a program that leaves them out, or rounds other values in their place, can miss the bound.
Values may be sent and summed in bfloat16 or wider, within the bound.
No kernel may reach another device: no remote copies, remote signals or barrier semaphores. Data moves between devices by JAX's collectives and lax.ppermute only.
A program may use at most 128 MiB of HBM per device.

```python
import math
import jax
import jax.numpy as jnp
from jax import lax

D = 5120
H = 40
HD = 128
S_POS = 640
BLK = 128
FRAMES = 32
TOKENS = 20480
NB = 5
HEADS_DEV = 5
TEMP_DEV = 2


def spread_gain(key, low_gain, high_gain):
    uniform_part = jax.random.uniform(key, (H * HD,), jnp.float32)
    return jnp.exp(math.log(low_gain) + uniform_part * (math.log(high_gain) - math.log(low_gain)))


def draw_q_gain(key, part):
    key = jax.random.fold_in(key, 11)
    return spread_gain(key, 0.5, 2.5)


def draw_k_gain(key, part):
    key = jax.random.fold_in(key, 17)
    return spread_gain(key, 0.5, 2.5)


def draw_head_kind(key, part):
    key = jax.random.fold_in(key, 23)
    groups = H // HEADS_DEV
    scores = jax.random.randint(key, (groups, HEADS_DEV), 0, 1 << 20) * HEADS_DEV + jnp.arange(HEADS_DEV, dtype=jnp.int32)[None, :]
    head_rank = jnp.argsort(jnp.argsort(scores, axis=1, stable=True), axis=1, stable=True)
    return (head_rank < TEMP_DEV).astype(jnp.int32).reshape(H)


def draw_block_live(key, part):
    key = jax.random.fold_in(key, 37)
    reach_key, roll_key = jax.random.split(key)
    reach_keys = jax.random.randint(reach_key, (FRAMES, 1, 1, 1), 1, NB + 1)
    roll_keys = jax.random.randint(roll_key, (FRAMES, H, NB, NB), 0, NB)
    diagonal = (jnp.arange(NB)[:, None] == jnp.arange(NB)[None, :])[None, None]
    return jnp.logical_or(roll_keys < reach_keys, diagonal).astype(jnp.int32)


def block_levels(rng, dims, shards, smallest, top_value):
    level = 1.0
    for axis_at, parts in shards:
        steps = jax.random.uniform(jax.random.fold_in(jax.random.fold_in(rng, 6), axis_at), (parts,), jnp.float32, smallest / len(shards), top_value / len(shards))
        level = level * jnp.repeat(jnp.exp(steps), dims[axis_at] // parts).reshape((-1,) + (1,) * (len(dims) - 1 - axis_at))
    return level


def bell_draw(key, shape, spread, most, pieces=(), held_as=jnp.bfloat16):
    result = jax.random.normal(key, shape, jnp.float32) * spread
    if len(pieces) > 0:
        result = block_levels(key, shape, pieces, -0.22, 0.18) * result
    return jnp.clip(result, min=-most, max=most).astype(held_as)


def setup_inputs(seed: int = 0) -> dict:
    keys = jax.random.split(jax.random.key(seed), 7)
    return {
        "x_tokens": bell_draw(keys[0], (TOKENS, D), 1.0, 6.0, ((0, 32), (1, 8))),
        "w_qkv": bell_draw(keys[1], (3, D, H * HD), D ** -0.5, 0.078125, ((1, 32), (2, 8))),
        "q_gain": draw_q_gain(jax.random.fold_in(keys[6], 71), 0),
        "k_gain": draw_k_gain(jax.random.fold_in(keys[6], 71), 0),
        "head_kind": draw_head_kind(jax.random.fold_in(keys[6], 71), 0),
        "block_live": draw_block_live(jax.random.fold_in(keys[6], 71), 0),
    }


def softmax_rows(scores):
    row_max = lax.optimization_barrier(jnp.max(scores, axis=-1, keepdims=True))
    expo = jnp.exp(scores - row_max)
    return (expo / lax.optimization_barrier(jnp.sum(expo, axis=-1, keepdims=True))).astype(jnp.bfloat16)

def normalize(raw_rows, gain):
    mean_sq = lax.optimization_barrier(jnp.mean(raw_rows * raw_rows, axis=-1, keepdims=True))
    return (raw_rows * lax.rsqrt(mean_sq + 1e-06) * gain).astype(jnp.bfloat16)

def reference(x_tokens, w_qkv, q_gain, k_gain, head_kind, block_live):
    score_scale = 1.0 / math.sqrt(HD)
    queries = normalize(jnp.dot(x_tokens, w_qkv[0], preferred_element_type=jnp.float32), q_gain)
    keys_n = normalize(jnp.dot(x_tokens, w_qkv[1], preferred_element_type=jnp.float32), k_gain)
    values = jnp.dot(x_tokens, w_qkv[2], preferred_element_type=jnp.float32).astype(jnp.bfloat16)
    grid_shape = (FRAMES, S_POS, H, HD)
    query_grid = queries.reshape(grid_shape)
    key_grid = keys_n.reshape(grid_shape)
    value_grid = values.reshape(grid_shape)

    def spatial_frame(frame_args):
        frame_q, frame_k, frame_v, frame_live = frame_args
        scores = jnp.einsum('qhd,khd->hqk', frame_q.astype(jnp.float32), frame_k.astype(jnp.float32)) * score_scale
        key_mask = jnp.repeat(jnp.repeat(frame_live, BLK, axis=1), BLK, axis=2)
        scores = jnp.where(key_mask > 0, scores, -1e+30)
        sp_weights = softmax_rows(scores)
        return jnp.einsum('hqk,khd->qhd', sp_weights.astype(jnp.float32), frame_v.astype(jnp.float32)).astype(jnp.bfloat16)
    spatial = lax.map(spatial_frame, (query_grid, key_grid, value_grid, block_live))
    scores = jnp.einsum('fphd,gphd->phfg', query_grid.astype(jnp.float32), key_grid.astype(jnp.float32)) * score_scale
    tm_weights = softmax_rows(scores)
    temporal = jnp.einsum('phfg,gphd->fphd', tm_weights.astype(jnp.float32), value_grid.astype(jnp.float32)).astype(jnp.bfloat16)
    is_temporal = (head_kind > 0)[None, None, :, None]
    return jnp.where(is_temporal, temporal, spatial).reshape(TOKENS, H * HD)
```

```python
import functools
import math

import jax
import jax.numpy as jnp
from jax import lax
from jax.experimental import pallas as pl
from jax.experimental.pallas import tpu as pltpu
from jax.sharding import Mesh, PartitionSpec as P

D = 5120
HD = 128
BLK = 128
NB = 5
HEADS = 5
TEMP = 2
NZ = 8
NY = 4
ROWS = 160
TOK = 640
FEAT = 640
SCALE = 1.0 / math.sqrt(HD)
VMEM_LIMIT = 48 * 1024 * 1024


def hop(block, axis, size, step):
    return lax.ppermute(block, axis, [(i, (i + step) % size) for i in range(size)])


def ring_z(block, last_up):
    found = {0: block}
    up = down = block
    for step in range(1, 4):
        up = hop(up, "z", NZ, 1)
        down = hop(down, "z", NZ, -1)
        found[NZ - step] = up
        found[step] = down
    found[4] = hop(up, "z", NZ, 1) if last_up else hop(down, "z", NZ, -1)
    return found


def ring_y(block, last_up):
    up = hop(block, "y", NY, 1)
    down = hop(block, "y", NY, -1)
    far = hop(up, "y", NY, 1) if last_up else hop(down, "y", NY, -1)
    return {0: block, 3: up, 1: down, 2: far}


def gather_z_first(block, last_up):
    found = ring_z(block, last_up)
    pieces = []
    for turn, offsets in enumerate(((0, 1, 7, 2), (6, 3, 5, 4))):
        four = jnp.stack([found[o] for o in offsets])
        for y_off, part in ring_y(four, turn == 0).items():
            pieces.append((part, [(o, y_off) for o in offsets]))
    return pieces


def gather_y_first(block, last_up):
    found = ring_y(block, last_up)
    y_offsets = (0, 3, 1, 2)
    four = jnp.stack([found[o] for o in y_offsets])
    pieces = []
    for z_off, part in ring_z(four, last_up).items():
        pieces.append((part, [(z_off, o) for o in y_offsets]))
    return pieces


def project(tokens, pieces, splits):
    arrays = [part for part, _ in pieces]
    offsets = [where for _, where in pieces]
    width = arrays[0].shape[-1]
    count = len(arrays)

    def kernel(*refs):
        x_hbm = refs[0]
        w_hbm = refs[1 : 1 + count]
        outs = refs[1 + count : 1 + count + len(splits)]
        x_v, w_v, acc, x_sem, w_sem = refs[1 + count + len(splits) :]
        z = lax.axis_index("z")
        y = lax.axis_index("y")
        x_copies = []
        w_copies = {}
        for rel in range(NZ):
            z_at = lax.rem(z + rel, NZ)
            x_copies.append(pltpu.make_async_copy(x_hbm.at[z_at], x_v.at[rel], x_sem.at[rel]))
        for n in range(count):
            for m, (z_off, y_off) in enumerate(offsets[n]):
                y_at = lax.rem(y + y_off, NY)
                w_copies[z_off, y_off] = pltpu.make_async_copy(
                    w_hbm[n].at[m], w_v.at[z_off, y_at], w_sem.at[z_off, y_off]
                )
        for rel in range(NZ):
            x_copies[rel].start()
            for y_off in range(NY):
                w_copies[rel, y_off].start()
        for rel in range(NZ):
            x_copies[rel].wait()
            for y_off in range(NY):
                w_copies[rel, y_off].wait()
            part = jnp.dot(
                x_v[rel],
                w_v[rel].reshape(NY * ROWS, width),
                preferred_element_type=jnp.float32,
            )
            if rel == 0:
                acc[...] = part
            else:
                acc[...] += part
        start = 0
        for out, (cols, dtype, by_head) in zip(outs, splits):
            if by_head:
                for head in range(cols // HD):
                    at = start + head * HD
                    out[head] = acc[:, at : at + HD].astype(dtype)
            else:
                out[...] = acc[:, start : start + cols].astype(dtype)
            start += cols

    shapes = [
        jax.ShapeDtypeStruct((cols // HD, TOK, HD) if by_head else (TOK, cols), dtype)
        for cols, dtype, by_head in splits
    ]
    return pl.pallas_call(
        kernel,
        out_shape=shapes,
        in_specs=[pl.BlockSpec(memory_space=pl.ANY)] * (1 + count),
        out_specs=[pl.BlockSpec(memory_space=pltpu.VMEM)] * len(splits),
        scratch_shapes=[
            pltpu.VMEM((NZ, TOK, FEAT), jnp.bfloat16),
            pltpu.VMEM((NZ, NY, ROWS, width), jnp.bfloat16),
            pltpu.VMEM((TOK, width), jnp.float32),
            pltpu.SemaphoreType.DMA((NZ,)),
            pltpu.SemaphoreType.DMA((NZ, NY)),
        ],
        compiler_params=pltpu.CompilerParams(vmem_limit_bytes=VMEM_LIMIT),
        cost_estimate=pl.CostEstimate(
            flops=2 * TOK * D * width, bytes_accessed=2 * D * (TOK + width), transcendentals=0
        ),
    )(tokens, *arrays)


def softmax_rows(scores):
    row_max = jnp.max(scores, axis=-1, keepdims=True)
    expo = jnp.exp(scores - row_max)
    return (expo / jnp.sum(expo, axis=-1, keepdims=True)).astype(jnp.bfloat16)


def score_dot(left, right):
    return lax.dot_general(
        left, right, (((1,), (1,)), ((), ())), preferred_element_type=jnp.float32
    )


def spatial_attend(order, live, queries, keys_n, values):
    count = HEADS - TEMP

    def kernel(order_ref, live_ref, q_ref, k_ref, v_ref, out_ref):
        head = order_ref[TEMP + pl.program_id(0)]
        keys = k_ref[0]
        vals = v_ref[0]
        for qb in range(NB):
            rows = pl.ds(qb * BLK, BLK)
            scores = score_dot(q_ref[0, rows, :], keys) * SCALE
            parts = []
            for kb in range(NB):
                seen = live_ref[(head * NB + qb) * NB + kb] > 0
                parts.append(jnp.where(seen, scores[:, kb * BLK : (kb + 1) * BLK], -1e30))
            weights = softmax_rows(jnp.concatenate(parts, axis=1))
            out_ref[rows, :] = jnp.dot(
                weights, vals, preferred_element_type=jnp.float32
            ).astype(jnp.bfloat16)

    spec = pl.BlockSpec((1, TOK, HD), lambda i, order, live: (i, 0, 0))
    return pl.pallas_call(
        kernel,
        out_shape=jax.ShapeDtypeStruct((TOK, HEADS * HD), jnp.bfloat16),
        grid_spec=pltpu.PrefetchScalarGridSpec(
            num_scalar_prefetch=2,
            grid=(count,),
            in_specs=[spec, spec, spec],
            out_specs=pl.BlockSpec((TOK, HD), lambda i, order, live: (0, order[TEMP + i])),
        ),
        compiler_params=pltpu.CompilerParams(vmem_limit_bytes=VMEM_LIMIT),
        cost_estimate=pl.CostEstimate(
            flops=4 * count * TOK * TOK * HD, bytes_accessed=8 * count * TOK * HD,
            transcendentals=count * TOK * TOK,
        ),
    )(order, live, queries, keys_n, values)


def put_temporal(order, attended, temporal):
    def kernel(order_ref, base_ref, t_ref, out_ref):
        out_ref[...] = t_ref[0]

    return pl.pallas_call(
        kernel,
        out_shape=jax.ShapeDtypeStruct(attended.shape, attended.dtype),
        grid_spec=pltpu.PrefetchScalarGridSpec(
            num_scalar_prefetch=1,
            grid=(TEMP,),
            in_specs=[
                pl.BlockSpec(memory_space=pl.ANY),
                pl.BlockSpec((1, TOK, HD), lambda i, order: (i, 0, 0)),
            ],
            out_specs=pl.BlockSpec((TOK, HD), lambda i, order: (0, order[i])),
        ),
        input_output_aliases={1: 0},
    )(order, attended, temporal)


def temporal_attend(queries, keys_n, values):
    frames, places, _ = queries.shape
    group = 8
    rows = frames * group

    def kernel(q_ref, k_ref, v_ref, out_ref):
        row_at = lax.broadcasted_iota(jnp.int32, (rows, rows), 0)
        col_at = lax.broadcasted_iota(jnp.int32, (rows, rows), 1)
        same = lax.rem(row_at, group) == lax.rem(col_at, group)
        whole = [r[...].astype(jnp.float32) for r in (q_ref, k_ref, v_ref)]
        done = []
        for g in range(places // group):
            q, k, v = [
                a[:, g * group : (g + 1) * group, :].reshape(rows, HD).astype(jnp.bfloat16)
                for a in whole
            ]
            scores = jnp.where(same, score_dot(q, k) * SCALE, -1e30)
            weights = softmax_rows(scores)
            part = jnp.dot(weights, v, preferred_element_type=jnp.float32)
            done.append(part.reshape(frames, group, HD))
        out_ref[...] = jnp.concatenate(done, axis=1).astype(jnp.bfloat16)

    vmem = pl.BlockSpec(memory_space=pltpu.VMEM)
    return pl.pallas_call(
        kernel,
        out_shape=jax.ShapeDtypeStruct(queries.shape, jnp.bfloat16),
        in_specs=[vmem] * 3,
        out_specs=vmem,
        compiler_params=pltpu.CompilerParams(vmem_limit_bytes=VMEM_LIMIT),
        cost_estimate=pl.CostEstimate(
            flops=4 * rows * rows * HD * 5, bytes_accessed=8 * frames * places * HD,
            transcendentals=rows * rows * 5,
        ),
    )(queries, keys_n, values)


def head_order(head_kind):
    is_temp = head_kind > 0
    before_t = jnp.cumsum(is_temp.astype(jnp.int32)) - is_temp
    before_s = jnp.arange(HEADS) - before_t
    slot = jnp.where(is_temp, before_t, TEMP + before_s)
    hit = slot[None, :] == jnp.arange(HEADS)[:, None]
    return jnp.sum(jnp.where(hit, jnp.arange(HEADS)[None, :], 0), axis=1).astype(jnp.int32)


def pick_heads(array, heads):
    return [
        lax.dynamic_slice_in_dim(array, head * HD, HD, axis=array.ndim - 1) for head in heads
    ]


def shards(x_tokens, w_qkv, q_gain, k_gain, head_kind, block_live):
    order = head_order(head_kind)
    slots = [order[i] for i in range(HEADS)]
    tokens = lax.all_gather(x_tokens, ("x", "c"), axis=0)
    v_parts = pick_heads(w_qkv[2], slots)
    first = jnp.concatenate([w_qkv[0]] + v_parts[:TEMP], axis=1)
    third = jnp.concatenate(v_parts[TEMP:], axis=1)
    q_pieces = gather_z_first(first, True)
    k_pieces = gather_y_first(w_qkv[1], False)
    v_pieces = gather_y_first(third, True)
    q_raw, v_temp = project(
        tokens, q_pieces, [(HEADS * HD, jnp.float32, False), (TEMP * HD, jnp.bfloat16, True)]
    )
    (k_raw,) = project(tokens, k_pieces, [(HEADS * HD, jnp.float32, False)])
    (v_spat,) = project(tokens, v_pieces, [((HEADS - TEMP) * HD, jnp.bfloat16, True)])

    squares = jnp.stack([jnp.sum(q_raw * q_raw, axis=1), jnp.sum(k_raw * k_raw, axis=1)])
    squares = squares + hop(squares, "c", 2, 1)
    squares = squares + hop(squares, "x", 4, 1) + hop(squares, "x", 4, -1) + hop(squares, "x", 4, 2)
    factor = lax.rsqrt(squares / D + 1e-06)[:, :, None]

    def norm(raw, row, gain):
        heads = [
            (cols * factor[row] * scale).astype(jnp.bfloat16)
            for cols, scale in zip(pick_heads(raw, slots), pick_heads(gain, slots))
        ]
        return jnp.stack(heads[:TEMP]), jnp.stack(heads[TEMP:])

    q_temp, q_spat = norm(q_raw, 0, q_gain)
    k_temp, k_spat = norm(k_raw, 1, k_gain)

    def swap(array):
        return lax.all_to_all(array, ("z", "y"), split_axis=0, concat_axis=0, tiled=True)

    places = TEMP * TOK // (NZ * NY)
    moved_v = swap(v_temp.reshape(NZ * NY, places, HD))
    moved_q = swap(q_temp.reshape(NZ * NY, places, HD))
    moved_k = swap(k_temp.reshape(NZ * NY, places, HD))
    temporal = swap(temporal_attend(moved_q, moved_k, moved_v)).reshape(TEMP, TOK, HD)
    spatial = spatial_attend(order, block_live.reshape(-1), q_spat, k_spat, v_spat)
    return put_temporal(order, spatial, temporal)


def solution(mesh):
    fine = Mesh(mesh.devices.reshape(NZ, NY, 4, 2), ("z", "y", "x", "c"))
    seq, fsdp = ("z", "y"), ("x", "c")
    placed = (
        P(seq, fsdp),
        P(None, seq, fsdp),
        P(fsdp),
        P(fsdp),
        P(fsdp),
        P(seq, fsdp, None, None),
    )
    return jax.shard_map(
        shards, mesh=fine, in_specs=placed, out_specs=P(seq, fsdp), check_vma=False
    )
```

```python
import functools
import math

import jax
import jax.numpy as jnp
from jax import lax
from jax.experimental import pallas as pl
from jax.experimental.pallas import tpu as pltpu
from jax.sharding import Mesh, PartitionSpec as P

D = 5120
HD = 128
BLK = 128
NB = 5
HEADS = 5
TEMP = 2
NZ = 8
NY = 4
ROWS = 160
TOK = 640
FEAT = 640
SCALE = 1.0 / math.sqrt(HD)
VMEM_LIMIT = 56 * 1024 * 1024
Y_OFFSETS = (0, 3, 1, 2)
GROUPS = ((0, 1, 7), (2, 6), (3, 5, 4))


def hop(block, axis, size, step):
    return lax.ppermute(block, axis, [(i, (i + step) % size) for i in range(size)])


def ring_z(block):
    found = {0: block}
    up = down = block
    for step in range(1, 4):
        up = hop(up, "z", NZ, 1)
        down = hop(down, "z", NZ, -1)
        found[NZ - step] = up
        found[step] = down
    half = block.shape[0] // 2
    found[4] = (hop(up[:half], "z", NZ, 1), hop(down[half:], "z", NZ, -1))
    return found


def hop_y_by_core(block):
    pairs = []
    for y in range(NY):
        pairs.append((y * 2, ((y + 1) % NY) * 2))
        pairs.append((y * 2 + 1, ((y + NY - 1) % NY) * 2 + 1))
    return lax.ppermute(block, ("y", "c"), pairs)


def together(*arrays):
    return lax.optimization_barrier(arrays)


def gather_both(first, second, early, late):
    f_up, f_down = hop(first, "z", NZ, 1), hop(first, "z", NZ, -1)
    s_up, s_down = hop(second, "y", NY, 1), hop(second, "y", NY, -1)
    f_up, f_down, s_up, s_down, early = together(f_up, f_down, s_up, s_down, early)
    by_z = {0: first, 7: f_up, 1: f_down}
    turns = [[jnp.stack([by_z[o] for o in GROUPS[0]])]]

    s_far = hop(s_up, "y", NY, 1)
    f_up, f_down = hop(f_up, "z", NZ, 1), hop(f_down, "z", NZ, -1)
    hopped = hop_y_by_core(turns[0][0])
    s_far, f_up, f_down, hopped, late = together(s_far, f_up, f_down, hopped, late)
    turns[0].append(hopped)
    by_z[6], by_z[2] = f_up, f_down

    found = ring_z(jnp.stack([second, s_up, s_down, s_far]))
    f_up, f_down = hop(f_up, "z", NZ, 1), hop(f_down, "z", NZ, -1)
    by_z[5], by_z[3] = f_up, f_down
    half = ROWS // 2
    by_z[4] = jnp.concatenate([hop(f_up[:half], "z", NZ, 1), hop(f_down[half:], "z", NZ, -1)])
    for offsets in GROUPS[1:]:
        turns.append([jnp.stack([by_z[o] for o in offsets])])
    for turn in turns:
        while len(turn) < NY:
            turn.append(hop_y_by_core(turn[-1]))
    return turns, found, early, late


def copy_all(x_hbm, x_v, x_sem, w_moves, w_v, w_sem, slots):
    moves = []
    for slot, z_at in enumerate(slots):
        cols = pl.ds(slot * FEAT, FEAT)
        moves.append(pltpu.make_async_copy(x_hbm.at[z_at], x_v.at[:, cols], x_sem.at[slot]))
        for n, (src, y_at) in enumerate(w_moves[slot]):
            moves.append(pltpu.make_async_copy(src, w_v.at[slot, y_at], w_sem.at[slot, n]))
    for move in moves:
        move.start()
    return moves


def project(tokens, arrays, where, splits):
    width = arrays[0].shape[-1]
    count = len(arrays)

    def kernel(*refs):
        x_hbm = refs[0]
        w_hbm = refs[1 : 1 + count]
        at = 1 + count
        outs = refs[at : at + len(splits)]
        x_v, w_v, acc, x_sem, w_sem = refs[at + len(splits) :]
        z = lax.axis_index("z")
        y = lax.axis_index("y")
        turn = 2 * lax.axis_index("c") - 1
        w_moves = [
            [
                (w_hbm[n].at[m], lax.rem(y + NY + y_off + turn * hops, NY))
                for n, m, y_off, hops in where[z_off]
            ]
            for z_off in range(NZ)
        ]
        slots = [lax.rem(z + z_off, NZ) for z_off in range(NZ)]
        moves = copy_all(x_hbm, x_v, x_sem, w_moves, w_v, w_sem, slots)
        half = TOK // 2
        per = NZ // 2
        for part in range(2):
            for move in moves[part * per * (NY + 1) : (part + 1) * per * (NY + 1)]:
                move.wait()

            def body(step, carry):
                rows = pl.ds(pl.multiple_of(step * half, half), half)
                total = jnp.dot(
                    x_v[rows, part * per * FEAT : (part + 1) * per * FEAT],
                    w_v[part * per : (part + 1) * per].reshape(per * NY * ROWS, width),
                    preferred_element_type=jnp.float32,
                )
                if part == 0:
                    acc[rows, :] = total
                    return carry
                total = total + acc[rows, :]
                start = 0
                for out, (cols, dtype, by_head) in zip(outs, splits):
                    if by_head:
                        for head in range(cols // HD):
                            left = start + head * HD
                            out[head, rows, :] = total[:, left : left + HD].astype(dtype)
                    else:
                        out[rows, :] = total[:, start : start + cols].astype(dtype)
                    start += cols
                return carry

            lax.fori_loop(0, 2, body, 0)

    shapes = [
        jax.ShapeDtypeStruct((cols // HD, TOK, HD) if by_head else (TOK, cols), dtype)
        for cols, dtype, by_head in splits
    ]
    vmem = pl.BlockSpec(memory_space=pltpu.VMEM)
    return pl.pallas_call(
        kernel,
        out_shape=shapes,
        in_specs=[pl.BlockSpec(memory_space=pl.ANY)] * (1 + count),
        out_specs=[vmem] * len(splits),
        scratch_shapes=[
            pltpu.VMEM((TOK, D), jnp.bfloat16),
            pltpu.VMEM((NZ, NY, ROWS, width), jnp.bfloat16),
            pltpu.VMEM((TOK, width), jnp.float32),
            pltpu.SemaphoreType.DMA((NZ,)),
            pltpu.SemaphoreType.DMA((NZ, NY)),
        ],
        compiler_params=pltpu.CompilerParams(vmem_limit_bytes=VMEM_LIMIT),
        cost_estimate=pl.CostEstimate(
            flops=2 * TOK * D * width, bytes_accessed=2 * D * (TOK + width), transcendentals=0
        ),
    )(tokens, *arrays)


def project_z_first(tokens, turns, groups, splits):
    arrays = []
    where = {}
    for parts, offsets in zip(turns, groups):
        for m, z_off in enumerate(offsets):
            where[z_off] = [(len(arrays) + hops, m, 0, hops) for hops in range(NY)]
        arrays.extend(parts)
    return project(tokens, arrays, where, splits)


def project_y_first(tokens, found, splits):
    arrays = []
    where = {}
    for z_off, part in found.items():
        if z_off == 4:
            per = NY // 2
            where[4] = [
                (len(arrays) + m // per, m % per, o, 0) for m, o in enumerate(Y_OFFSETS)
            ]
            arrays.extend(part)
        else:
            where[z_off] = [(len(arrays), m, o, 0) for m, o in enumerate(Y_OFFSETS)]
            arrays.append(part)
    return project(tokens, arrays, where, splits)


def split_weights(head_kind, w_qkv):
    def kernel(kind_ref, w_ref, first_ref, second_ref, third_ref):
        first_ref[:, : HEADS * HD] = w_ref[0]
        second_ref[...] = w_ref[1]
        temp = jnp.int32(0)
        spat = jnp.int32(0)
        slots = [jnp.int32(0)] * HEADS
        for head in range(HEADS):
            is_temp = kind_ref[head] > 0
            slot = jnp.where(is_temp, temp, TEMP + spat)
            for n in range(HEADS):
                slots[n] = jnp.where(slot == n, head, slots[n])
            temp = temp + jnp.where(is_temp, 1, 0)
            spat = spat + jnp.where(is_temp, 0, 1)
        for n in range(HEADS):
            cols = w_ref[2, :, pl.ds(pl.multiple_of(slots[n] * HD, HD), HD)]
            if n < TEMP:
                at = (HEADS + n) * HD
                first_ref[:, at : at + HD] = cols
            else:
                at = (n - TEMP) * HD
                third_ref[:, at : at + HD] = cols

    vmem = pl.BlockSpec(memory_space=pltpu.VMEM)
    return pl.pallas_call(
        kernel,
        out_shape=[
            jax.ShapeDtypeStruct((ROWS, (HEADS + TEMP) * HD), jnp.bfloat16),
            jax.ShapeDtypeStruct((ROWS, HEADS * HD), jnp.bfloat16),
            jax.ShapeDtypeStruct((ROWS, (HEADS - TEMP) * HD), jnp.bfloat16),
        ],
        in_specs=[pl.BlockSpec(memory_space=pltpu.SMEM), vmem],
        out_specs=[vmem, vmem, vmem],
        compiler_params=pltpu.CompilerParams(vmem_limit_bytes=VMEM_LIMIT),
    )(head_kind, w_qkv)


def softmax_rows(scores):
    row_max = jnp.max(scores, axis=-1, keepdims=True)
    expo = jnp.exp(scores - row_max)
    return (expo / jnp.sum(expo, axis=-1, keepdims=True)).astype(jnp.bfloat16)


def score_dot(left, right):
    return lax.dot_general(
        left, right, (((1,), (1,)), ((), ())), preferred_element_type=jnp.float32
    )


def spatial_weights(order, live, queries, keys_n):
    count = HEADS - TEMP

    def kernel(order_ref, live_ref, q_ref, k_ref, out_ref):
        head = order_ref[TEMP + pl.program_id(0)]
        keys = k_ref[0]
        for qb in range(NB):
            rows = pl.ds(qb * BLK, BLK)
            scores = score_dot(q_ref[0, rows, :], keys) * SCALE
            parts = []
            for kb in range(NB):
                seen = live_ref[(head * NB + qb) * NB + kb] > 0
                parts.append(jnp.where(seen, scores[:, kb * BLK : (kb + 1) * BLK], -1e30))
            out_ref[0, rows, :] = softmax_rows(jnp.concatenate(parts, axis=1))

    spec = pl.BlockSpec((1, TOK, HD), lambda i, order, live: (i, 0, 0))
    return pl.pallas_call(
        kernel,
        out_shape=jax.ShapeDtypeStruct((count, TOK, TOK), jnp.bfloat16),
        grid_spec=pltpu.PrefetchScalarGridSpec(
            num_scalar_prefetch=2,
            grid=(count,),
            in_specs=[spec, spec],
            out_specs=pl.BlockSpec((1, TOK, TOK), lambda i, order, live: (i, 0, 0)),
        ),
        compiler_params=pltpu.CompilerParams(vmem_limit_bytes=VMEM_LIMIT),
        cost_estimate=pl.CostEstimate(
            flops=2 * count * TOK * TOK * HD, bytes_accessed=8 * count * TOK * TOK,
            transcendentals=count * TOK * TOK,
        ),
    )(order, live, queries, keys_n)


def spatial_values(order, tokens, rows_all, weights):
    count = HEADS - TEMP
    width = count * HD

    def kernel(order_ref, x_hbm, w_hbm, p_ref, out_ref, x_v, w_v, values, x_sem, w_sem):
        w_moves = [[(w_hbm.at[z * NY + n], n) for n in range(NY)] for z in range(NZ)]
        moves = copy_all(x_hbm, x_v, x_sem, w_moves, w_v, w_sem, list(range(NZ)))
        for move in moves:
            move.wait()
        values[...] = jnp.dot(
            x_v[...], w_v[...].reshape(D, width), preferred_element_type=jnp.float32
        ).astype(jnp.bfloat16)
        for n in range(count):
            cols = pl.ds(pl.multiple_of(order_ref[TEMP + n] * HD, HD), HD)
            out_ref[:, cols] = jnp.dot(
                p_ref[n], values[:, n * HD : (n + 1) * HD], preferred_element_type=jnp.float32
            ).astype(jnp.bfloat16)

    any_spec = pl.BlockSpec(memory_space=pl.ANY)
    vmem = pl.BlockSpec(memory_space=pltpu.VMEM)
    return pl.pallas_call(
        kernel,
        out_shape=jax.ShapeDtypeStruct((TOK, HEADS * HD), jnp.bfloat16),
        in_specs=[pl.BlockSpec(memory_space=pltpu.SMEM), any_spec, any_spec, vmem],
        out_specs=vmem,
        scratch_shapes=[
            pltpu.VMEM((TOK, D), jnp.bfloat16),
            pltpu.VMEM((NZ, NY, ROWS, width), jnp.bfloat16),
            pltpu.VMEM((TOK, width), jnp.bfloat16),
            pltpu.SemaphoreType.DMA((NZ,)),
            pltpu.SemaphoreType.DMA((NZ, NY)),
        ],
        compiler_params=pltpu.CompilerParams(vmem_limit_bytes=VMEM_LIMIT),
        cost_estimate=pl.CostEstimate(
            flops=2 * TOK * D * width + 2 * count * TOK * TOK * HD,
            bytes_accessed=2 * D * (TOK + width),
            transcendentals=0,
        ),
    )(order, tokens, rows_all, weights)


def put_temporal(order, attended, temporal):
    def kernel(order_ref, base_ref, t_ref, out_ref):
        out_ref[...] = t_ref[0]

    return pl.pallas_call(
        kernel,
        out_shape=jax.ShapeDtypeStruct(attended.shape, attended.dtype),
        grid_spec=pltpu.PrefetchScalarGridSpec(
            num_scalar_prefetch=1,
            grid=(TEMP,),
            in_specs=[
                pl.BlockSpec(memory_space=pl.ANY),
                pl.BlockSpec((1, TOK, HD), lambda i, order: (i, 0, 0)),
            ],
            out_specs=pl.BlockSpec((TOK, HD), lambda i, order: (0, order[i])),
        ),
        input_output_aliases={1: 0},
    )(order, attended, temporal)


def temporal_attend(queries, keys_n, values):
    frames, places, _ = queries.shape
    group = 8
    rows = frames * group

    def kernel(q_ref, k_ref, v_ref, out_ref):
        row_at = lax.broadcasted_iota(jnp.int32, (rows, rows), 0)
        col_at = lax.broadcasted_iota(jnp.int32, (rows, rows), 1)
        same = lax.rem(row_at, group) == lax.rem(col_at, group)
        whole = [r[...].astype(jnp.float32) for r in (q_ref, k_ref, v_ref)]
        done = []
        for g in range(places // group):
            q, k, v = [
                a[:, g * group : (g + 1) * group, :].reshape(rows, HD).astype(jnp.bfloat16)
                for a in whole
            ]
            scores = jnp.where(same, score_dot(q, k) * SCALE, -1e30)
            weights = softmax_rows(scores)
            part = jnp.dot(weights, v, preferred_element_type=jnp.float32)
            done.append(part.reshape(frames, group, HD))
        out_ref[...] = jnp.concatenate(done, axis=1).astype(jnp.bfloat16)

    vmem = pl.BlockSpec(memory_space=pltpu.VMEM)
    return pl.pallas_call(
        kernel,
        out_shape=jax.ShapeDtypeStruct(queries.shape, jnp.bfloat16),
        in_specs=[vmem] * 3,
        out_specs=vmem,
        compiler_params=pltpu.CompilerParams(vmem_limit_bytes=VMEM_LIMIT),
        cost_estimate=pl.CostEstimate(
            flops=4 * rows * rows * HD * 5, bytes_accessed=8 * frames * places * HD,
            transcendentals=rows * rows * 5,
        ),
    )(queries, keys_n, values)


def head_order(head_kind):
    is_temp = head_kind > 0
    before_t = jnp.cumsum(is_temp.astype(jnp.int32)) - is_temp
    before_s = jnp.arange(HEADS) - before_t
    slot = jnp.where(is_temp, before_t, TEMP + before_s)
    hit = slot[None, :] == jnp.arange(HEADS)[:, None]
    return jnp.sum(jnp.where(hit, jnp.arange(HEADS)[None, :], 0), axis=1).astype(jnp.int32)


def pick_heads(array, heads):
    return [
        lax.dynamic_slice_in_dim(array, head * HD, HD, axis=array.ndim - 1) for head in heads
    ]


def shards(x_tokens, w_qkv, q_gain, k_gain, head_kind, block_live):
    first, second, third = split_weights(head_kind, w_qkv)
    order = head_order(head_kind)
    slots = [order[i] for i in range(HEADS)]
    q_turns, k_found, x_tokens, third = gather_both(first, second, x_tokens, third)
    tokens = lax.all_gather(x_tokens, ("x", "c"), axis=0)
    third_all = lax.all_gather(third, ("z", "y"), axis=0)
    q_raw, v_temp = project_z_first(
        tokens,
        q_turns,
        GROUPS,
        [(HEADS * HD, jnp.float32, False), (TEMP * HD, jnp.bfloat16, True)],
    )
    (k_raw,) = project_y_first(tokens, k_found, [(HEADS * HD, jnp.float32, False)])

    def swap(array):
        return lax.all_to_all(array, ("z", "y"), split_axis=0, concat_axis=0, tiled=True)

    places = TEMP * TOK // (NZ * NY)
    moved_v = swap(v_temp.reshape(NZ * NY, places, HD))
    squares = jnp.stack([jnp.sum(q_raw * q_raw, axis=1), jnp.sum(k_raw * k_raw, axis=1)])
    squares, moved_v = together(squares, moved_v)
    squares = squares + hop(squares, "c", 2, 1)
    squares = squares + hop(squares, "x", 4, 1) + hop(squares, "x", 4, -1) + hop(squares, "x", 4, 2)
    factor = lax.rsqrt(squares / D + 1e-06)[:, :, None]

    def norm(raw, row, gain):
        heads = [
            (cols * factor[row] * scale).astype(jnp.bfloat16)
            for cols, scale in zip(pick_heads(raw, slots), pick_heads(gain, slots))
        ]
        return jnp.stack(heads[:TEMP]), jnp.stack(heads[TEMP:])

    q_temp, q_spat = norm(q_raw, 0, q_gain)
    k_temp, k_spat = norm(k_raw, 1, k_gain)

    both = [a.reshape(NZ * NY, places, HD) for a in (q_temp, k_temp)]
    moved = swap(jnp.concatenate(both, axis=1))
    weights = spatial_weights(order, block_live.reshape(-1), q_spat, k_spat)
    spatial = spatial_values(order, tokens, third_all, weights)
    moved, spatial = together(moved, spatial)
    moved_q, moved_k = moved[:, :places], moved[:, places:]
    temporal = swap(temporal_attend(moved_q, moved_k, moved_v)).reshape(TEMP, TOK, HD)
    return put_temporal(order, spatial, temporal)


def solution(mesh):
    fine = Mesh(mesh.devices.reshape(NZ, NY, 4, 2), ("z", "y", "x", "c"))
    seq, fsdp = ("z", "y"), ("x", "c")
    placed = (
        P(seq, fsdp),
        P(None, seq, fsdp),
        P(fsdp),
        P(fsdp),
        P(fsdp),
        P(seq, fsdp, None, None),
    )
    return jax.shard_map(
        shards, mesh=fine, in_specs=placed, out_specs=P(seq, fsdp), check_vma=False
    )
```

```python
import functools
import math

import jax
import jax.numpy as jnp
from jax import lax
from jax.experimental import pallas as pl
from jax.experimental.pallas import tpu as pltpu
from jax.sharding import Mesh, PartitionSpec as P

D = 5120
HD = 128
BLK = 128
NB = 5
HEADS = 5
TEMP = 2
PLACES = 40
NZ = 8
NY = 4
ROWS = 160
TOK = 640
FEAT = 640
SCALE = 1.0 / math.sqrt(HD)
VMEM_LIMIT = 56 * 1024 * 1024
Y_OFFSETS = (0, 3, 1, 2)
GROUPS = ((0, 1, 7), (2, 6), (3, 5, 4))


def hop(block, axis, size, step):
    return lax.ppermute(block, axis, [(i, (i + step) % size) for i in range(size)])


def hop_y_by_core(block):
    pairs = []
    for y in range(NY):
        pairs.append((y * 2, ((y + 1) % NY) * 2))
        pairs.append((y * 2 + 1, ((y + NY - 1) % NY) * 2 + 1))
    return lax.ppermute(block, ("y", "c"), pairs)


def together(*arrays):
    return lax.optimization_barrier(arrays)


def gather_both(first, second, late):
    def hop_both(up, down):
        return hop(up, "z", NZ, 1), hop(down, "z", NZ, -1)

    by_z = {0: first}

    def group(offsets):
        return [jnp.stack([by_z[o] for o in offsets])]

    def advance(turn):
        turn.append(hop_y_by_core(turn[-1]))

    up, down = hop_both(first, first)
    s_up, s_down = hop(second, "y", NY, 1), hop(second, "y", NY, -1)
    up, down, s_up, s_down, late = together(up, down, s_up, s_down, late)
    by_z[7], by_z[1] = up, down

    near = group(GROUPS[0])
    advance(near)
    s_far = hop(s_up, "y", NY, 1)
    up, down = hop_both(up, down)
    s_far, up, down, near[1] = together(s_far, up, down, near[1])
    by_z[6], by_z[2] = up, down

    middle = group(GROUPS[1])
    advance(near)
    advance(middle)
    up, down = hop_both(up, down)
    up, down, near[2], middle[1] = together(up, down, near[2], middle[1])
    by_z[5], by_z[3] = up, down

    found = {0: jnp.stack([second, s_up, s_down, s_far])}
    half = ROWS // 2
    by_z[4] = jnp.concatenate(hop_both(up[:half], down[half:]))
    up, down = hop_both(found[0], found[0])
    advance(near)
    advance(middle)
    up, down, near[3], middle[2], by_z[4] = together(up, down, near[3], middle[2], by_z[4])
    found[7], found[1] = up, down

    far = group(GROUPS[2])
    advance(far)
    advance(middle)
    up, down = hop_both(up, down)
    up, down, far[1], middle[3] = together(up, down, far[1], middle[3])
    found[6], found[2] = up, down
    up, down = hop_both(up, down)
    found[5], found[3] = up, down
    half = NY // 2
    found[4] = hop_both(up[:half], down[half:])
    advance(far)
    advance(far)
    return [near, middle, far], found, late


def copy_all(x_hbm, x_v, x_sem, w_moves, w_v, w_sem, slots):
    moves = []
    for slot, z_at in enumerate(slots):
        cols = pl.ds(slot * FEAT, FEAT)
        moves.append(pltpu.make_async_copy(x_hbm.at[z_at], x_v.at[:, cols], x_sem.at[slot]))
        for n, (src, y_at) in enumerate(w_moves[slot]):
            moves.append(pltpu.make_async_copy(src, w_v.at[slot, y_at], w_sem.at[slot, n]))
    for move in moves:
        move.start()
    return moves


def project(tokens, arrays, where, splits, relative=True):
    width = arrays[0].shape[-1]
    count = len(arrays)

    def kernel(*refs):
        x_hbm = refs[0]
        w_hbm = refs[1 : 1 + count]
        at = 1 + count
        outs = refs[at : at + len(splits)]
        x_v, w_v, acc, x_sem, w_sem = refs[at + len(splits) :]
        z = lax.axis_index("z") if relative else 0
        y = lax.axis_index("y") if relative else 0
        turn = 2 * lax.axis_index("c") - 1
        w_moves = [
            [
                (w_hbm[n].at[m], lax.rem(y + NY + y_off + turn * hops, NY))
                for n, m, y_off, hops in where[z_off]
            ]
            for z_off in range(NZ)
        ]
        slots = [lax.rem(z + z_off, NZ) for z_off in range(NZ)]
        moves = copy_all(x_hbm, x_v, x_sem, w_moves, w_v, w_sem, slots)
        half = TOK // 2
        per = NZ // 2
        for part in range(2):
            for move in moves[part * per * (NY + 1) : (part + 1) * per * (NY + 1)]:
                move.wait()

            def body(step, carry):
                rows = pl.ds(pl.multiple_of(step * half, half), half)
                total = jnp.dot(
                    x_v[rows, part * per * FEAT : (part + 1) * per * FEAT],
                    w_v[part * per : (part + 1) * per].reshape(per * NY * ROWS, width),
                    preferred_element_type=jnp.float32,
                )
                if part == 0:
                    acc[rows, :] = total
                    return carry
                total = total + acc[rows, :]
                start = 0
                for out, (cols, dtype, by_head) in zip(outs, splits):
                    if by_head:
                        for head in range(cols // HD):
                            left = start + head * HD
                            out[head, rows, :] = total[:, left : left + HD].astype(dtype)
                    else:
                        out[rows, :] = total[:, start : start + cols].astype(dtype)
                    start += cols
                return carry

            lax.fori_loop(0, 2, body, 0)

    shapes = [
        jax.ShapeDtypeStruct((cols // HD, TOK, HD) if by_head else (TOK, cols), dtype)
        for cols, dtype, by_head in splits
    ]
    vmem = pl.BlockSpec(memory_space=pltpu.VMEM)
    return pl.pallas_call(
        kernel,
        out_shape=shapes,
        in_specs=[pl.BlockSpec(memory_space=pl.ANY)] * (1 + count),
        out_specs=[vmem] * len(splits),
        scratch_shapes=[
            pltpu.VMEM((TOK, D), jnp.bfloat16),
            pltpu.VMEM((NZ, NY, ROWS, width), jnp.bfloat16),
            pltpu.VMEM((TOK, width), jnp.float32),
            pltpu.SemaphoreType.DMA((NZ,)),
            pltpu.SemaphoreType.DMA((NZ, NY)),
        ],
        compiler_params=pltpu.CompilerParams(vmem_limit_bytes=VMEM_LIMIT),
        cost_estimate=pl.CostEstimate(
            flops=2 * TOK * D * width, bytes_accessed=2 * D * (TOK + width), transcendentals=0
        ),
    )(tokens, *arrays)


def project_both(tokens, turns, found):
    arrays = []
    q_where = {}
    k_where = {}
    for parts, group in zip(turns, GROUPS):
        for m, z_off in enumerate(group):
            q_where[z_off] = [(len(arrays) + hops, m, 0, hops) for hops in range(NY)]
        arrays.extend(parts)
    for z_off, part in found.items():
        pieces = part if z_off == 4 else (part,)
        per = NY // len(pieces)
        k_where[z_off] = [
            (len(arrays) + m // per, m % per, o, 0) for m, o in enumerate(Y_OFFSETS)
        ]
        arrays.extend(pieces)
    count = len(arrays)
    q_cols = HEADS * HD
    left = arrays[0].shape[-1]
    width = left + q_cols
    per = NZ // 2

    def kernel(*refs):
        x_hbm = refs[0]
        w_hbm = refs[1 : 1 + count]
        q_out, k_out, v_out, sums_out, x_v, w_v, acc, x_sem, w_sem = refs[1 + count :]
        z = lax.axis_index("z")
        y = lax.axis_index("y")
        turn = 2 * lax.axis_index("c") - 1
        moves = []
        for slot in range(NZ):
            z_at = lax.rem(z + slot, NZ)
            cols = pl.ds(slot * FEAT, FEAT)
            found_moves = [
                pltpu.make_async_copy(x_hbm.at[z_at], x_v.at[:, cols], x_sem.at[slot])
            ]
            for side, where in enumerate((q_where, k_where)):
                cols = pl.ds(0, left) if side == 0 else pl.ds(left, q_cols)
                for i, (n, m, y_off, hops) in enumerate(where[slot]):
                    y_at = lax.rem(y + NY + y_off + turn * hops, NY)
                    found_moves.append(
                        pltpu.make_async_copy(
                            w_hbm[n].at[m],
                            w_v.at[slot, y_at, :, cols],
                            w_sem.at[slot, side * NY + i],
                        )
                    )
            for move in found_moves:
                move.start()
            moves.append(found_moves)

        def half(part):
            for found_moves in moves[part * per : (part + 1) * per]:
                for move in found_moves:
                    move.wait()
            return jnp.dot(
                x_v[:, part * per * FEAT : (part + 1) * per * FEAT],
                w_v[part * per : (part + 1) * per].reshape(per * NY * ROWS, width),
                preferred_element_type=jnp.float32,
            )

        acc[...] = half(0)
        acc[...] += half(1)
        sums_out[...] = jnp.zeros_like(sums_out)
        for n, (out, start) in enumerate(((q_out, 0), (k_out, left))):
            raw = acc[:, start : start + q_cols]
            out[...] = raw
            sums = jnp.sum(raw * raw, axis=1, keepdims=True)
            sums_out[n : n + 1, :] = jnp.transpose(jnp.broadcast_to(sums, (TOK, HD)))[:1, :]
        for head in range(TEMP):
            start = q_cols + head * HD
            v_out[head] = acc[:, start : start + HD].astype(jnp.bfloat16)

    vmem = pl.BlockSpec(memory_space=pltpu.VMEM)
    return pl.pallas_call(
        kernel,
        out_shape=[
            jax.ShapeDtypeStruct((TOK, q_cols), jnp.float32),
            jax.ShapeDtypeStruct((TOK, q_cols), jnp.float32),
            jax.ShapeDtypeStruct((TEMP, TOK, HD), jnp.bfloat16),
            jax.ShapeDtypeStruct((8, TOK), jnp.float32),
        ],
        in_specs=[pl.BlockSpec(memory_space=pl.ANY)] * (1 + count),
        out_specs=[vmem] * 4,
        scratch_shapes=[
            pltpu.VMEM((TOK, D), jnp.bfloat16),
            pltpu.VMEM((NZ, NY, ROWS, width), jnp.bfloat16),
            pltpu.VMEM((TOK, width), jnp.float32),
            pltpu.SemaphoreType.DMA((NZ,)),
            pltpu.SemaphoreType.DMA((NZ, 2 * NY)),
        ],
        compiler_params=pltpu.CompilerParams(vmem_limit_bytes=VMEM_LIMIT),
        cost_estimate=pl.CostEstimate(
            flops=2 * TOK * D * width, bytes_accessed=2 * D * (TOK + width), transcendentals=0
        ),
    )(tokens, *arrays)


def project_gathered(tokens, rows_all, splits):
    where = {z: [(0, z * NY + y, y, 0) for y in range(NY)] for z in range(NZ)}
    return project(tokens, [rows_all], where, splits, relative=False)


def split_weights(head_kind, w_qkv):
    def kernel(kind_ref, w_ref, first_ref, second_ref, third_ref):
        first_ref[:, : HEADS * HD] = w_ref[0]
        second_ref[...] = w_ref[1]
        temp = jnp.int32(0)
        spat = jnp.int32(0)
        slots = [jnp.int32(0)] * HEADS
        for head in range(HEADS):
            is_temp = kind_ref[head] > 0
            slot = jnp.where(is_temp, temp, TEMP + spat)
            for n in range(HEADS):
                slots[n] = jnp.where(slot == n, head, slots[n])
            temp = temp + jnp.where(is_temp, 1, 0)
            spat = spat + jnp.where(is_temp, 0, 1)
        for n in range(HEADS):
            cols = w_ref[2, :, pl.ds(pl.multiple_of(slots[n] * HD, HD), HD)]
            if n < TEMP:
                at = (HEADS + n) * HD
                first_ref[:, at : at + HD] = cols
            else:
                at = (n - TEMP) * HD
                third_ref[:, at : at + HD] = cols

    vmem = pl.BlockSpec(memory_space=pltpu.VMEM)
    return pl.pallas_call(
        kernel,
        out_shape=[
            jax.ShapeDtypeStruct((ROWS, (HEADS + TEMP) * HD), jnp.bfloat16),
            jax.ShapeDtypeStruct((ROWS, HEADS * HD), jnp.bfloat16),
            jax.ShapeDtypeStruct((ROWS, (HEADS - TEMP) * HD), jnp.bfloat16),
        ],
        in_specs=[pl.BlockSpec(memory_space=pltpu.SMEM), vmem],
        out_specs=[vmem, vmem, vmem],
        compiler_params=pltpu.CompilerParams(vmem_limit_bytes=VMEM_LIMIT),
    )(head_kind, w_qkv)


def softmax_rows(scores):
    row_max = jnp.max(scores, axis=-1, keepdims=True)
    expo = jnp.exp(scores - row_max)
    return (expo / jnp.sum(expo, axis=-1, keepdims=True)).astype(jnp.bfloat16)


def score_dot(left, right):
    return lax.dot_general(
        left, right, (((1,), (1,)), ((), ())), preferred_element_type=jnp.float32
    )


def spatial_attend(order, live, queries, keys_n, values):
    def kernel(order_ref, live_ref, q_ref, k_ref, v_ref, out_ref):
        head = order_ref[TEMP + pl.program_id(0)]
        for qb in range(NB):
            rows = pl.ds(qb * BLK, BLK)
            scores = score_dot(q_ref[0, rows, :], k_ref[0]) * SCALE
            parts = []
            for kb in range(NB):
                seen = live_ref[(head * NB + qb) * NB + kb] > 0
                parts.append(jnp.where(seen, scores[:, kb * BLK : (kb + 1) * BLK], -1e30))
            weights = softmax_rows(jnp.concatenate(parts, axis=1))
            out_ref[rows, :] = jnp.dot(
                weights, v_ref[0], preferred_element_type=jnp.float32
            ).astype(jnp.bfloat16)

    spec = pl.BlockSpec((1, TOK, HD), lambda i, order, live: (i, 0, 0))
    return pl.pallas_call(
        kernel,
        out_shape=jax.ShapeDtypeStruct((TOK, HEADS * HD), jnp.bfloat16),
        grid_spec=pltpu.PrefetchScalarGridSpec(
            num_scalar_prefetch=2,
            grid=((HEADS - TEMP),),
            in_specs=[spec, spec, spec],
            out_specs=pl.BlockSpec((TOK, HD), lambda i, order, live: (0, order[TEMP + i])),
        ),
        compiler_params=pltpu.CompilerParams(vmem_limit_bytes=VMEM_LIMIT),
        cost_estimate=pl.CostEstimate(
            flops=4 * (HEADS - TEMP) * TOK * TOK * HD, bytes_accessed=8 * (HEADS - TEMP) * TOK * HD,
            transcendentals=(HEADS - TEMP) * TOK * TOK,
        ),
    )(order, live, queries, keys_n, values)


def put_temporal(order, attended, temporal):
    def kernel(order_ref, base_ref, t_ref, out_ref):
        out_ref[...] = t_ref[0]

    return pl.pallas_call(
        kernel,
        out_shape=jax.ShapeDtypeStruct(attended.shape, attended.dtype),
        grid_spec=pltpu.PrefetchScalarGridSpec(
            num_scalar_prefetch=1,
            grid=(TEMP,),
            in_specs=[
                pl.BlockSpec(memory_space=pl.ANY),
                pl.BlockSpec((1, TOK, HD), lambda i, order: (i, 0, 0)),
            ],
            out_specs=pl.BlockSpec((TOK, HD), lambda i, order: (0, order[i])),
        ),
        input_output_aliases={1: 0},
    )(order, attended, temporal)


def temporal_attend(moved, values):
    frames, places, _ = values.shape
    group = 8
    rows = frames * group

    def kernel(both_ref, v_ref, out_ref):
        row_at = lax.broadcasted_iota(jnp.int32, (rows, rows), 0)
        col_at = lax.broadcasted_iota(jnp.int32, (rows, rows), 1)
        same = lax.rem(row_at, group) == lax.rem(col_at, group)
        both = both_ref[...].astype(jnp.float32)
        whole = (both[:, :places], both[:, places:], v_ref[...].astype(jnp.float32))
        done = []
        for g in range(places // group):
            q, k, v = [
                a[:, g * group : (g + 1) * group, :].reshape(rows, HD).astype(jnp.bfloat16)
                for a in whole
            ]
            scores = jnp.where(same, score_dot(q, k) * SCALE, -1e30)
            weights = softmax_rows(scores)
            part = jnp.dot(weights, v, preferred_element_type=jnp.float32)
            done.append(part.reshape(frames, group, HD))
        out_ref[...] = jnp.concatenate(done, axis=1).astype(jnp.bfloat16)

    vmem = pl.BlockSpec(memory_space=pltpu.VMEM)
    return pl.pallas_call(
        kernel,
        out_shape=jax.ShapeDtypeStruct(values.shape, jnp.bfloat16),
        in_specs=[vmem] * 2,
        out_specs=vmem,
        compiler_params=pltpu.CompilerParams(vmem_limit_bytes=VMEM_LIMIT),
        cost_estimate=pl.CostEstimate(
            flops=4 * rows * rows * HD * 5, bytes_accessed=8 * frames * places * HD,
            transcendentals=rows * rows * 5,
        ),
    )(moved, values)


def head_order(head_kind):
    is_temp = head_kind > 0
    before_t = jnp.cumsum(is_temp.astype(jnp.int32)) - is_temp
    before_s = jnp.arange(HEADS) - before_t
    slot = jnp.where(is_temp, before_t, TEMP + before_s)
    hit = slot[None, :] == jnp.arange(HEADS)[:, None]
    return jnp.sum(jnp.where(hit, jnp.arange(HEADS)[None, :], 0), axis=1).astype(jnp.int32)


def normalize(order, squares, q_raw, k_raw, q_gain, k_gain):
    def kernel(order_ref, s_ref, q_ref, k_ref, q_gain_ref, k_gain_ref, both, q_spat, k_spat):
        factor = lax.rsqrt(jnp.transpose(s_ref[...]) / D + 1e-06)
        sides = ((q_ref, q_gain_ref, q_spat), (k_ref, k_gain_ref, k_spat))
        for n, (raw, gain, spat) in enumerate(sides):
            for slot in range(HEADS):
                cols = pl.ds(pl.multiple_of(order_ref[slot] * HD, HD), HD)
                value = raw[:, cols] * factor[:, n : n + 1] * gain[:, cols]
                if slot < TEMP:
                    across = TOK // PLACES
                    into = pl.ds(slot * across, across)
                    both[into, n * PLACES : (n + 1) * PLACES, :] = value.reshape(
                        across, PLACES, HD
                    ).astype(jnp.bfloat16)
                else:
                    spat[slot - TEMP] = value.astype(jnp.bfloat16)

    vmem = pl.BlockSpec(memory_space=pltpu.VMEM)
    return pl.pallas_call(
        kernel,
        out_shape=[
            jax.ShapeDtypeStruct((NZ * NY, 2 * PLACES, HD), jnp.bfloat16),
            jax.ShapeDtypeStruct((HEADS - TEMP, TOK, HD), jnp.bfloat16),
            jax.ShapeDtypeStruct((HEADS - TEMP, TOK, HD), jnp.bfloat16),
        ],
        in_specs=[pl.BlockSpec(memory_space=pltpu.SMEM)] + [vmem] * 5,
        out_specs=[vmem] * 3,
        compiler_params=pltpu.CompilerParams(vmem_limit_bytes=VMEM_LIMIT),
        cost_estimate=pl.CostEstimate(
            flops=6 * TOK * HEADS * HD, bytes_accessed=12 * TOK * HEADS * HD, transcendentals=TOK
        ),
    )(order, squares, q_raw, k_raw, q_gain[None, :], k_gain[None, :])


def swap(array):
    return lax.all_to_all(array, ("z", "y"), split_axis=0, concat_axis=0, tiled=True)


def shards(x_tokens, w_qkv, q_gain, k_gain, head_kind, block_live):
    first, second, third = split_weights(head_kind, w_qkv)
    order = head_order(head_kind)
    tokens = lax.all_gather(x_tokens, ("x", "c"), axis=0)
    q_turns, k_found, third = gather_both(first, second, third)
    third_all = lax.all_gather(third, ("z", "y"), axis=0)
    q_raw, k_raw, v_temp, squares = project_both(tokens, q_turns, k_found)
    squares = squares + hop(squares, "c", 2, 1)
    squares = squares + hop(squares, "x", 4, 1) + hop(squares, "x", 4, -1) + hop(squares, "x", 4, 2)
    moved_v = swap(v_temp.reshape(NZ * NY, PLACES, HD))
    squares, moved_v = together(squares, moved_v)
    both, q_spat, k_spat = normalize(order, squares, q_raw, k_raw, q_gain, k_gain)
    moved = swap(both)
    (v_spat,) = project_gathered(tokens, third_all, [((HEADS - TEMP) * HD, jnp.bfloat16, True)])
    moved, v_spat = together(moved, v_spat)
    temporal = swap(temporal_attend(moved, moved_v)).reshape(TEMP, TOK, HD)
    spatial = spatial_attend(order, block_live.reshape(-1), q_spat, k_spat, v_spat)
    return put_temporal(order, spatial, temporal)


def solution(mesh):
    fine = Mesh(mesh.devices.reshape(NZ, NY, 4, 2), ("z", "y", "x", "c"))
    seq, fsdp = ("z", "y"), ("x", "c")
    placed = (
        P(seq, fsdp),
        P(None, seq, fsdp),
        P(fsdp),
        P(fsdp),
        P(fsdp),
        P(seq, fsdp, None, None),
    )
    return jax.shard_map(
        shards, mesh=fine, in_specs=placed, out_specs=P(seq, fsdp), check_vma=False
    )
```

```python
import functools
import math

import jax
import jax.numpy as jnp
from jax import lax
from jax.experimental import pallas as pl
from jax.experimental.pallas import tpu as pltpu
from jax.sharding import Mesh, PartitionSpec as P

D = 5120
HD = 128
BLK = 128
NB = 5
HEADS = 5
TEMP = 2
PLACES = 40
NZ = 8
NY = 4
ROWS = 160
TOK = 640
FEAT = 640
SCALE = 1.0 / math.sqrt(HD)
VMEM_LIMIT = 56 * 1024 * 1024
Y_OFFSETS = (0, 3, 1, 2)
GROUPS = ((0, 1, 7), (2, 6), (3, 5, 4))


def hop(block, axis, size, step):
    return lax.ppermute(block, axis, [(i, (i + step) % size) for i in range(size)])


def hop_y_by_core(block):
    pairs = []
    for y in range(NY):
        pairs.append((y * 2, ((y + 1) % NY) * 2))
        pairs.append((y * 2 + 1, ((y + NY - 1) % NY) * 2 + 1))
    return lax.ppermute(block, ("y", "c"), pairs)


def together(*arrays):
    return lax.optimization_barrier(arrays)


def gather_both(first, second, late, tokens):
    def hop_both(up, down):
        return hop(up, "z", NZ, 1), hop(down, "z", NZ, -1)

    by_z = {0: first}

    def group(offsets):
        return [jnp.stack([by_z[o] for o in offsets])]

    def advance(turn):
        turn.append(hop_y_by_core(turn[-1]))

    up, down = hop_both(first, first)
    s_up, s_down = hop(second, "y", NY, 1), hop(second, "y", NY, -1)
    up, down, s_up, s_down, late = together(up, down, s_up, s_down, late)
    by_z[7], by_z[1] = up, down

    near = group(GROUPS[0])
    advance(near)
    s_far = hop(s_up, "y", NY, 1)
    up, down = hop_both(up, down)
    s_far, up, down, near[1] = together(s_far, up, down, near[1])
    by_z[6], by_z[2] = up, down

    middle = group(GROUPS[1])
    advance(near)
    advance(middle)
    up, down = hop_both(up, down)
    up, down, near[2], middle[1] = together(up, down, near[2], middle[1])
    by_z[5], by_z[3] = up, down

    found = {0: jnp.stack([second, s_up, s_down, s_far])}
    half = ROWS // 2
    by_z[4] = jnp.concatenate(hop_both(up[:half], down[half:]))
    up, down = hop_both(found[0], found[0])
    advance(near)
    advance(middle)
    up, down, near[3], middle[2], by_z[4] = together(up, down, near[3], middle[2], by_z[4])
    found[7], found[1] = up, down

    far = group(GROUPS[2])
    advance(far)
    advance(middle)
    up, down = hop_both(up, down)
    up, down, far[1], middle[3] = together(up, down, far[1], middle[3])
    found[6], found[2] = up, down
    up, down = hop_both(up, down)
    (base,) = project_both(tokens, [near, middle], found, GROUPS[:2], None)
    advance(far)
    up, down, base, far[2] = together(up, down, base, far[2])
    found[5], found[3] = up, down
    half = NY // 2
    found[4] = hop_both(up[:half], down[half:])
    advance(far)
    return [far], found, late, base


def copy_all(x_hbm, x_v, x_sem, w_moves, w_v, w_sem, slots):
    moves = []
    for slot, z_at in enumerate(slots):
        cols = pl.ds(slot * FEAT, FEAT)
        moves.append(pltpu.make_async_copy(x_hbm.at[z_at], x_v.at[:, cols], x_sem.at[slot]))
        for n, (src, y_at) in enumerate(w_moves[slot]):
            moves.append(pltpu.make_async_copy(src, w_v.at[slot, y_at], w_sem.at[slot, n]))
    for move in moves:
        move.start()
    return moves


def project(tokens, arrays, where, splits, relative=True):
    width = arrays[0].shape[-1]
    count = len(arrays)

    def kernel(*refs):
        x_hbm = refs[0]
        w_hbm = refs[1 : 1 + count]
        at = 1 + count
        outs = refs[at : at + len(splits)]
        x_v, w_v, acc, x_sem, w_sem = refs[at + len(splits) :]
        z = lax.axis_index("z") if relative else 0
        y = lax.axis_index("y") if relative else 0
        turn = 2 * lax.axis_index("c") - 1
        w_moves = [
            [
                (w_hbm[n].at[m], lax.rem(y + NY + y_off + turn * hops, NY))
                for n, m, y_off, hops in where[z_off]
            ]
            for z_off in range(NZ)
        ]
        slots = [lax.rem(z + z_off, NZ) for z_off in range(NZ)]
        moves = copy_all(x_hbm, x_v, x_sem, w_moves, w_v, w_sem, slots)
        half = TOK // 2
        per = NZ // 2
        for part in range(2):
            for move in moves[part * per * (NY + 1) : (part + 1) * per * (NY + 1)]:
                move.wait()

            def body(step, carry):
                rows = pl.ds(pl.multiple_of(step * half, half), half)
                total = jnp.dot(
                    x_v[rows, part * per * FEAT : (part + 1) * per * FEAT],
                    w_v[part * per : (part + 1) * per].reshape(per * NY * ROWS, width),
                    preferred_element_type=jnp.float32,
                )
                if part == 0:
                    acc[rows, :] = total
                    return carry
                total = total + acc[rows, :]
                start = 0
                for out, (cols, dtype, by_head) in zip(outs, splits):
                    if by_head:
                        for head in range(cols // HD):
                            left = start + head * HD
                            out[head, rows, :] = total[:, left : left + HD].astype(dtype)
                    else:
                        out[rows, :] = total[:, start : start + cols].astype(dtype)
                    start += cols
                return carry

            lax.fori_loop(0, 2, body, 0)

    shapes = [
        jax.ShapeDtypeStruct((cols // HD, TOK, HD) if by_head else (TOK, cols), dtype)
        for cols, dtype, by_head in splits
    ]
    vmem = pl.BlockSpec(memory_space=pltpu.VMEM)
    return pl.pallas_call(
        kernel,
        out_shape=shapes,
        in_specs=[pl.BlockSpec(memory_space=pl.ANY)] * (1 + count),
        out_specs=[vmem] * len(splits),
        scratch_shapes=[
            pltpu.VMEM((TOK, D), jnp.bfloat16),
            pltpu.VMEM((NZ, NY, ROWS, width), jnp.bfloat16),
            pltpu.VMEM((TOK, width), jnp.float32),
            pltpu.SemaphoreType.DMA((NZ,)),
            pltpu.SemaphoreType.DMA((NZ, NY)),
        ],
        compiler_params=pltpu.CompilerParams(vmem_limit_bytes=VMEM_LIMIT),
        cost_estimate=pl.CostEstimate(
            flops=2 * TOK * D * width, bytes_accessed=2 * D * (TOK + width), transcendentals=0
        ),
    )(tokens, *arrays)


def project_both(tokens, turns, found, groups, base):
    arrays = []
    q_where = {}
    k_where = {}
    offsets = [z_off for group in groups for z_off in group]
    n_slots = len(offsets)
    for parts, group in zip(turns, groups):
        for m, z_off in enumerate(group):
            q_where[z_off] = [(len(arrays) + hops, m, 0, hops) for hops in range(NY)]
        arrays.extend(parts)
    for z_off in offsets:
        pieces = found[z_off] if z_off == 4 else (found[z_off],)
        per = NY // len(pieces)
        k_where[z_off] = [
            (len(arrays) + m // per, m % per, o, 0) for m, o in enumerate(Y_OFFSETS)
        ]
        arrays.extend(pieces)
    count = len(arrays)
    q_cols = HEADS * HD
    left = arrays[0].shape[-1]
    width = left + q_cols
    last = base is not None
    if last:
        shapes = [
            jax.ShapeDtypeStruct((TOK, q_cols), jnp.float32),
            jax.ShapeDtypeStruct((TOK, q_cols), jnp.float32),
            jax.ShapeDtypeStruct((TEMP, TOK, HD), jnp.bfloat16),
            jax.ShapeDtypeStruct((8, TOK), jnp.float32),
        ]
    else:
        shapes = [jax.ShapeDtypeStruct((TOK, width), jnp.float32)]

    def kernel(*refs):
        x_hbm = refs[0]
        w_hbm = refs[1 : 1 + count]
        at = 1 + count + (1 if last else 0)
        outs = refs[at : at + len(shapes)]
        x_v, w_v, acc, x_sem, w_sem = refs[at + len(shapes) :]
        z = lax.axis_index("z")
        y = lax.axis_index("y")
        turn = 2 * lax.axis_index("c") - 1
        moves = []
        for slot, z_off in enumerate(offsets):
            z_at = lax.rem(z + z_off, NZ)
            cols = pl.ds(slot * FEAT, FEAT)
            found_moves = [
                pltpu.make_async_copy(x_hbm.at[z_at], x_v.at[:, cols], x_sem.at[slot])
            ]
            for side, where in enumerate((q_where, k_where)):
                cols = pl.ds(0, left) if side == 0 else pl.ds(left, q_cols)
                for i, (n, m, y_off, hops) in enumerate(where[z_off]):
                    y_at = lax.rem(y + NY + y_off + turn * hops, NY)
                    found_moves.append(
                        pltpu.make_async_copy(
                            w_hbm[n].at[m],
                            w_v.at[slot, y_at, :, cols],
                            w_sem.at[slot, side * NY + i],
                        )
                    )
            for move in found_moves:
                move.start()
            moves.append(found_moves)

        for found_moves in moves:
            for move in found_moves:
                move.wait()
        total = jnp.dot(
            x_v[...],
            w_v[...].reshape(n_slots * NY * ROWS, width),
            preferred_element_type=jnp.float32,
        )
        if not last:
            outs[0][...] = total
            return
        q_out, k_out, v_out, sums_out = outs
        acc[...] = refs[1 + count][...] + total
        sums_out[...] = jnp.zeros_like(sums_out)
        for n, (out, start) in enumerate(((q_out, 0), (k_out, left))):
            raw = acc[:, start : start + q_cols]
            out[...] = raw
            sums = jnp.sum(raw * raw, axis=1, keepdims=True)
            sums_out[n : n + 1, :] = jnp.transpose(jnp.broadcast_to(sums, (TOK, HD)))[:1, :]
        for head in range(TEMP):
            start = q_cols + head * HD
            v_out[head] = acc[:, start : start + HD].astype(jnp.bfloat16)

    vmem = pl.BlockSpec(memory_space=pltpu.VMEM)
    return pl.pallas_call(
        kernel,
        out_shape=shapes,
        in_specs=[pl.BlockSpec(memory_space=pl.ANY)] * (1 + count) + [vmem] * last,
        out_specs=[vmem] * len(shapes),
        scratch_shapes=[
            pltpu.VMEM((TOK, n_slots * FEAT), jnp.bfloat16),
            pltpu.VMEM((n_slots, NY, ROWS, width), jnp.bfloat16),
            pltpu.VMEM((TOK, width), jnp.float32),
            pltpu.SemaphoreType.DMA((n_slots,)),
            pltpu.SemaphoreType.DMA((n_slots, 2 * NY)),
        ],
        compiler_params=pltpu.CompilerParams(vmem_limit_bytes=VMEM_LIMIT),
        cost_estimate=pl.CostEstimate(
            flops=2 * TOK * n_slots * FEAT * width,
            bytes_accessed=2 * n_slots * FEAT * (TOK + width),
            transcendentals=0,
        ),
    )(tokens, *arrays, *([base] if last else []))


def project_gathered(tokens, rows_all, splits):
    where = {z: [(0, z * NY + y, y, 0) for y in range(NY)] for z in range(NZ)}
    return project(tokens, [rows_all], where, splits, relative=False)


def split_weights(head_kind, w_qkv):
    def kernel(kind_ref, w_ref, first_ref, second_ref, third_ref):
        first_ref[:, : HEADS * HD] = w_ref[0]
        second_ref[...] = w_ref[1]
        temp = jnp.int32(0)
        spat = jnp.int32(0)
        slots = [jnp.int32(0)] * HEADS
        for head in range(HEADS):
            is_temp = kind_ref[head] > 0
            slot = jnp.where(is_temp, temp, TEMP + spat)
            for n in range(HEADS):
                slots[n] = jnp.where(slot == n, head, slots[n])
            temp = temp + jnp.where(is_temp, 1, 0)
            spat = spat + jnp.where(is_temp, 0, 1)
        for n in range(HEADS):
            cols = w_ref[2, :, pl.ds(pl.multiple_of(slots[n] * HD, HD), HD)]
            if n < TEMP:
                at = (HEADS + n) * HD
                first_ref[:, at : at + HD] = cols
            else:
                at = (n - TEMP) * HD
                third_ref[:, at : at + HD] = cols

    vmem = pl.BlockSpec(memory_space=pltpu.VMEM)
    return pl.pallas_call(
        kernel,
        out_shape=[
            jax.ShapeDtypeStruct((ROWS, (HEADS + TEMP) * HD), jnp.bfloat16),
            jax.ShapeDtypeStruct((ROWS, HEADS * HD), jnp.bfloat16),
            jax.ShapeDtypeStruct((ROWS, (HEADS - TEMP) * HD), jnp.bfloat16),
        ],
        in_specs=[pl.BlockSpec(memory_space=pltpu.SMEM), vmem],
        out_specs=[vmem, vmem, vmem],
        compiler_params=pltpu.CompilerParams(vmem_limit_bytes=VMEM_LIMIT),
    )(head_kind, w_qkv)


def softmax_rows(scores):
    row_max = jnp.max(scores, axis=-1, keepdims=True)
    expo = jnp.exp(scores - row_max)
    return (expo / jnp.sum(expo, axis=-1, keepdims=True)).astype(jnp.bfloat16)


def score_dot(left, right):
    return lax.dot_general(
        left, right, (((1,), (1,)), ((), ())), preferred_element_type=jnp.float32
    )


def spatial_attend(order, live, queries, keys_n, values):
    def kernel(order_ref, live_ref, q_ref, k_ref, v_ref, out_ref):
        head = order_ref[TEMP + pl.program_id(0)]
        for qb in range(NB):
            rows = pl.ds(qb * BLK, BLK)
            scores = score_dot(q_ref[0, rows, :], k_ref[0]) * SCALE
            parts = []
            for kb in range(NB):
                seen = live_ref[(head * NB + qb) * NB + kb] > 0
                parts.append(jnp.where(seen, scores[:, kb * BLK : (kb + 1) * BLK], -1e30))
            weights = softmax_rows(jnp.concatenate(parts, axis=1))
            out_ref[rows, :] = jnp.dot(
                weights, v_ref[0], preferred_element_type=jnp.float32
            ).astype(jnp.bfloat16)

    spec = pl.BlockSpec((1, TOK, HD), lambda i, order, live: (i, 0, 0))
    return pl.pallas_call(
        kernel,
        out_shape=jax.ShapeDtypeStruct((TOK, HEADS * HD), jnp.bfloat16),
        grid_spec=pltpu.PrefetchScalarGridSpec(
            num_scalar_prefetch=2,
            grid=((HEADS - TEMP),),
            in_specs=[spec, spec, spec],
            out_specs=pl.BlockSpec((TOK, HD), lambda i, order, live: (0, order[TEMP + i])),
        ),
        compiler_params=pltpu.CompilerParams(vmem_limit_bytes=VMEM_LIMIT),
        cost_estimate=pl.CostEstimate(
            flops=4 * (HEADS - TEMP) * TOK * TOK * HD, bytes_accessed=8 * (HEADS - TEMP) * TOK * HD,
            transcendentals=(HEADS - TEMP) * TOK * TOK,
        ),
    )(order, live, queries, keys_n, values)


def put_temporal(order, attended, temporal):
    def kernel(order_ref, base_ref, t_ref, out_ref):
        out_ref[...] = t_ref[0]

    return pl.pallas_call(
        kernel,
        out_shape=jax.ShapeDtypeStruct(attended.shape, attended.dtype),
        grid_spec=pltpu.PrefetchScalarGridSpec(
            num_scalar_prefetch=1,
            grid=(TEMP,),
            in_specs=[
                pl.BlockSpec(memory_space=pl.ANY),
                pl.BlockSpec((1, TOK, HD), lambda i, order: (i, 0, 0)),
            ],
            out_specs=pl.BlockSpec((TOK, HD), lambda i, order: (0, order[i])),
        ),
        input_output_aliases={1: 0},
    )(order, attended, temporal)


def temporal_attend(moved, values):
    frames, places, _ = values.shape
    group = 8
    rows = frames * group

    def kernel(both_ref, v_ref, out_ref):
        row_at = lax.broadcasted_iota(jnp.int32, (rows, rows), 0)
        col_at = lax.broadcasted_iota(jnp.int32, (rows, rows), 1)
        same = lax.rem(row_at, group) == lax.rem(col_at, group)
        both = both_ref[...].astype(jnp.float32)
        whole = (both[:, :places], both[:, places:], v_ref[...].astype(jnp.float32))
        done = []
        for g in range(places // group):
            q, k, v = [
                a[:, g * group : (g + 1) * group, :].reshape(rows, HD).astype(jnp.bfloat16)
                for a in whole
            ]
            scores = jnp.where(same, score_dot(q, k) * SCALE, -1e30)
            weights = softmax_rows(scores)
            part = jnp.dot(weights, v, preferred_element_type=jnp.float32)
            done.append(part.reshape(frames, group, HD))
        out_ref[...] = jnp.concatenate(done, axis=1).astype(jnp.bfloat16)

    vmem = pl.BlockSpec(memory_space=pltpu.VMEM)
    return pl.pallas_call(
        kernel,
        out_shape=jax.ShapeDtypeStruct(values.shape, jnp.bfloat16),
        in_specs=[vmem] * 2,
        out_specs=vmem,
        compiler_params=pltpu.CompilerParams(vmem_limit_bytes=VMEM_LIMIT),
        cost_estimate=pl.CostEstimate(
            flops=4 * rows * rows * HD * 5, bytes_accessed=8 * frames * places * HD,
            transcendentals=rows * rows * 5,
        ),
    )(moved, values)


def head_order(head_kind):
    is_temp = head_kind > 0
    before_t = jnp.cumsum(is_temp.astype(jnp.int32)) - is_temp
    before_s = jnp.arange(HEADS) - before_t
    slot = jnp.where(is_temp, before_t, TEMP + before_s)
    hit = slot[None, :] == jnp.arange(HEADS)[:, None]
    return jnp.sum(jnp.where(hit, jnp.arange(HEADS)[None, :], 0), axis=1).astype(jnp.int32)


def normalize(order, squares, q_raw, k_raw, q_gain, k_gain):
    def kernel(order_ref, s_ref, q_ref, k_ref, q_gain_ref, k_gain_ref, both, q_spat, k_spat):
        factor = lax.rsqrt(jnp.transpose(s_ref[...]) / D + 1e-06)
        sides = ((q_ref, q_gain_ref, q_spat), (k_ref, k_gain_ref, k_spat))
        for n, (raw, gain, spat) in enumerate(sides):
            for slot in range(HEADS):
                cols = pl.ds(pl.multiple_of(order_ref[slot] * HD, HD), HD)
                value = raw[:, cols] * factor[:, n : n + 1] * gain[:, cols]
                if slot < TEMP:
                    across = TOK // PLACES
                    into = pl.ds(slot * across, across)
                    both[into, n * PLACES : (n + 1) * PLACES, :] = value.reshape(
                        across, PLACES, HD
                    ).astype(jnp.bfloat16)
                else:
                    spat[slot - TEMP] = value.astype(jnp.bfloat16)

    vmem = pl.BlockSpec(memory_space=pltpu.VMEM)
    return pl.pallas_call(
        kernel,
        out_shape=[
            jax.ShapeDtypeStruct((NZ * NY, 2 * PLACES, HD), jnp.bfloat16),
            jax.ShapeDtypeStruct((HEADS - TEMP, TOK, HD), jnp.bfloat16),
            jax.ShapeDtypeStruct((HEADS - TEMP, TOK, HD), jnp.bfloat16),
        ],
        in_specs=[pl.BlockSpec(memory_space=pltpu.SMEM)] + [vmem] * 5,
        out_specs=[vmem] * 3,
        compiler_params=pltpu.CompilerParams(vmem_limit_bytes=VMEM_LIMIT),
        cost_estimate=pl.CostEstimate(
            flops=6 * TOK * HEADS * HD, bytes_accessed=12 * TOK * HEADS * HD, transcendentals=TOK
        ),
    )(order, squares, q_raw, k_raw, q_gain[None, :], k_gain[None, :])


def swap(array):
    return lax.all_to_all(array, ("z", "y"), split_axis=0, concat_axis=0, tiled=True)


def shards(x_tokens, w_qkv, q_gain, k_gain, head_kind, block_live):
    first, second, third = split_weights(head_kind, w_qkv)
    order = head_order(head_kind)
    tokens = lax.all_gather(x_tokens, ("x", "c"), axis=0)
    q_turns, k_found, third, base = gather_both(first, second, third, tokens)
    third_all = lax.all_gather(third, ("z", "y"), axis=0)
    q_raw, k_raw, v_temp, squares = project_both(tokens, q_turns, k_found, GROUPS[2:], base)
    squares = squares + hop(squares, "c", 2, 1)
    squares = squares + hop(squares, "x", 4, 1) + hop(squares, "x", 4, -1) + hop(squares, "x", 4, 2)
    moved_v = swap(v_temp.reshape(NZ * NY, PLACES, HD))
    squares, moved_v = together(squares, moved_v)
    both, q_spat, k_spat = normalize(order, squares, q_raw, k_raw, q_gain, k_gain)
    moved = swap(both)
    (v_spat,) = project_gathered(tokens, third_all, [((HEADS - TEMP) * HD, jnp.bfloat16, True)])
    moved, v_spat = together(moved, v_spat)
    temporal = swap(temporal_attend(moved, moved_v)).reshape(TEMP, TOK, HD)
    spatial = spatial_attend(order, block_live.reshape(-1), q_spat, k_spat, v_spat)
    return put_temporal(order, spatial, temporal)


def solution(mesh):
    fine = Mesh(mesh.devices.reshape(NZ, NY, 4, 2), ("z", "y", "x", "c"))
    seq, fsdp = ("z", "y"), ("x", "c")
    placed = (
        P(seq, fsdp),
        P(None, seq, fsdp),
        P(fsdp),
        P(fsdp),
        P(fsdp),
        P(seq, fsdp, None, None),
    )
    return jax.shard_map(
        shards, mesh=fine, in_specs=placed, out_specs=P(seq, fsdp), check_vma=False
    )
```
